256 devices in a mesh: shot: 64 (over x, z, y_hi), xline: 4 (over y_lo, core).
Axes of the slice: x: 4, y: 4 (y_hi: 2, y_lo: 2; y = y_hi * 2 + y_lo), z: 8, core: 2. Of those that a mesh axis runs over, the one named last changes fastest.
Arguments:
- surface_gathers: bfloat16 [2, 8, 16, 4096, 512], P(None, None, 'xline', 'shot'), may hold values from -6 to 6
- source_gathers: bfloat16 [2, 8, 8192, 16, 320], P(None, None, 'shot', 'xline'), may hold values from -0.09375 to 0.09375
- aperture: int32 [8192, 2], P('shot'), may hold values from -128 to 4223, as said below
- live: int32 [16, 4096], P('xline', 'shot'), may hold values from 128 to 512
Outputs:
- predicted: bfloat16 [2, 8, 8192, 512], P(None, None, 'shot', 'xline')
The draws below stay inside these ranges and needn't reach their ends.
Inputs may be any that keep to these rules, and one draw needn't show every extreme that they name: Shot s with j = s % 128 sits at inline point c = (s // 128) * 64 + j % 64; aperture[s, 0] lies in c - 128 to c - 64, aperture[s, 1] in c + 64 to c + 128, both ends reached by the shots j = 0 and j = 127 of every block.
All inputs are finite; a program needn't handle non-finite values.
Results may differ from the reference program's by a relative error of at most 0.001.
Values may be sent and summed in bfloat16 or wider, within the bound.
No kernel may reach another device: no remote copies, remote signals or barrier semaphores. Data moves between devices by JAX's collectives and lax.ppermute only.
A program may use at most 192 MiB of HBM per device.

```python
import jax
import jax.numpy as jnp
from jax import lax

FREQS = 8
RECV = 512
SURFACE_POINTS = 64
APER = 256
S_DEV = 128
REACH = 2
SPREAD = 320
NI = 4096
KX = 16
NS = 8192
N_SHOT = 64


def draw_aperture(key, part):
    key = jax.random.fold_in(key, 11)
    leading_key, second_key = jax.random.split(key)
    shot_ids = jnp.arange(NS, dtype=jnp.int32)
    local_shot = shot_ids % S_DEV
    centre = shot_ids // S_DEV * SURFACE_POINTS + local_shot % SURFACE_POINTS
    low_cut = jax.random.randint(leading_key, (NS,), 0, APER // 4 + 1, dtype=jnp.int32)
    high_cut = jax.random.randint(second_key, (NS,), 0, APER // 4 + 1, dtype=jnp.int32)
    full_band = (local_shot == 0) | (local_shot == S_DEV - 1)
    low_cut = jnp.where(full_band, 0, low_cut)
    high_cut = jnp.where(full_band, 0, high_cut)
    begin = centre - APER // 2 + low_cut
    finish = centre + APER // 2 - high_cut
    return jnp.stack([begin, finish], axis=-1).astype(jnp.int32)


def draw_live(key, part):
    key = jax.random.fold_in(key, 23)
    counts = jax.random.randint(key, (KX, NI), RECV // 4, RECV + 1, dtype=jnp.int32)
    counts = counts.at[0, 0].set(RECV)
    counts = counts.at[KX - 1, NI - 1].set(RECV // 4)
    return counts.astype(jnp.int32)


def steps_of(key, shape, pieces, least, largest):
    def one(dim, blocks):
        steps = jax.random.uniform(jax.random.fold_in(jax.random.fold_in(key, 6), dim), (blocks,), jnp.float32, least / len(pieces), largest / len(pieces))
        return jnp.repeat(jnp.exp(steps), shape[dim] // blocks).reshape((-1,) + (1,) * (len(shape) - dim - 1))

    loudness = one(*pieces[0])
    for cut in pieces[1:]:
        loudness = loudness * one(*cut)
    return loudness


def bell_draw(stream_key, shape, scale, reach, pieces=(), kind=jnp.bfloat16):
    factor_of = steps_of(stream_key, shape, pieces, -0.22, 0.18) if pieces else 1.0
    values = jax.random.normal(stream_key, shape, jnp.float32) * scale * factor_of
    return jnp.minimum(jnp.maximum(values, -reach), reach).astype(kind)


def setup_inputs(seed: int = 0) -> dict:
    keys = jax.random.split(jax.random.key(seed), 5)
    return {
        "surface_gathers": bell_draw(keys[0], (2, FREQS, KX, NI, RECV), 1.0, 6.0, ((2, 4), (3, 64))),
        "source_gathers": bell_draw(keys[1], (2, FREQS, NS, KX, SPREAD), (APER * KX) ** -0.5, 0.09375, ((2, 64), (3, 4))),
        "aperture": draw_aperture(jax.random.fold_in(keys[4], 71), 0),
        "live": draw_live(jax.random.fold_in(keys[4], 71), 0),
    }


def contract(leading_operand, trailing_operand):
    return jnp.einsum("ginu,gnuw->giw", leading_operand, trailing_operand)


def reference(surface_gathers, source_gathers, aperture, live):
    receiver_ids = jnp.arange(RECV, dtype=jnp.int32)
    muted = jnp.where(receiver_ids[None, None, :] < live[:, :, None], surface_gathers, jnp.zeros((), surface_gathers.dtype))
    margin = REACH * SURFACE_POINTS
    padded = jnp.pad(muted, ((0, 0), (0, 0), (0, 0), (margin, margin), (0, 0)))
    spread_ids = jnp.arange(SPREAD, dtype=jnp.int32)

    def one_block(block_id):
        window = lax.dynamic_slice_in_dim(padded, (block_id * SURFACE_POINTS).astype(jnp.int32), SPREAD, 3).astype(jnp.float32)
        start = (block_id * S_DEV).astype(jnp.int32)
        block_shots = lax.dynamic_slice_in_dim(source_gathers, start, S_DEV, 2)
        band_rows = lax.dynamic_slice_in_dim(aperture, start, S_DEV, 0)
        inline = block_id * SURFACE_POINTS - margin + spread_ids
        inside = (inline[None, :] >= band_rows[:, 0:1]) & (inline[None, :] < band_rows[:, 1:2])
        masked = jnp.where(inside[None, None, :, None, :], block_shots, jnp.zeros((), block_shots.dtype)).astype(jnp.float32)
        real_part = contract(masked[0], window[0]) - contract(masked[1], window[1])
        imag_part = contract(masked[0], window[1]) + contract(masked[1], window[0])
        return jnp.stack([real_part, imag_part]).astype(jnp.bfloat16)

    predicted = lax.map(one_block, jnp.arange(N_SHOT, dtype=jnp.int32))
    return jnp.transpose(predicted, (1, 2, 0, 3, 4)).reshape(2, FREQS, NS, RECV)
```

```python
import functools

import jax
import jax.numpy as jnp
from jax import lax
from jax.experimental import pallas as pl
from jax.experimental.pallas import tpu as pltpu
from jax.sharding import Mesh, PartitionSpec as P

CHUNKS = (2, 2, 2, 2)
SHOT = ("sup", "half")
XLINE = ("side", "core")
RING = ("half", "side")


def shifted(block, distance):
    n = lax.axis_size("sup")
    return lax.ppermute(
        block, "sup", [(i, i + distance) for i in range(n) if 0 <= i + distance < n]
    )


def swapped(block, axis):
    return lax.ppermute(block, axis, [(0, 1), (1, 0)])


def products_kernel(place, below, here, above, own, cross, keep, send):
    half, core = place[0], place[1]
    upper = half == 1
    pts, recv = below.shape[3], below.shape[4]
    shots = own.shape[4]
    rows = below.shape[2] * pts

    def flat(values):
        return values.reshape(rows, shots)

    lefts = []
    for part in range(2):
        mine = [flat(own[part, 0, :, 2 * k * pts : (2 * k + 1) * pts, :]) for k in range(3)]
        low, high = (flat(cross[part, 0, :, k * pts : (k + 1) * pts, :]) for k in range(2))
        none = jnp.zeros_like(low)
        theirs = [
            jnp.where(upper, low, none),
            jnp.where(upper, high, low),
            jnp.where(upper, none, high),
        ]
        lefts.append([jnp.concatenate(pair, axis=1) for pair in zip(mine, theirs)])
    total = jnp.zeros((4 * shots, recv), jnp.float32)
    for k, window in enumerate((below, here, above)):
        real, imag = lefts[0][k], lefts[1][k]
        for part, left in enumerate(
            (jnp.concatenate([real, imag], axis=1), jnp.concatenate([-imag, real], axis=1))
        ):
            total += lax.dot_general(
                left,
                window[part, 0].reshape(rows, recv),
                (((0,), (0,)), ((), ())),
                preferred_element_type=jnp.float32,
            )
    width = recv // 4
    for side in range(2):
        even = total[:, 2 * side * width : (2 * side + 1) * width]
        odd = total[:, (2 * side + 1) * width : (2 * side + 2) * width]
        stays = jnp.where(core == 0, even, odd)
        leaves = jnp.where(core == 0, odd, even)
        for part in range(2):
            for block, to in enumerate((half, 1 - half)):
                first = (2 * part + block) * shots
                keep[to, side, part, 0] = stays[first : first + shots]
                send[to, side, part, 0] = leaves[first : first + shots]


def products(place, below, here, above, own, cross, first):
    freqs, xs, pts, recv = here.shape[1:]
    spread, shots = own.shape[3:]

    def of_freq(shape, offset=0):
        return pl.BlockSpec((2, 1) + shape, lambda f: (0, f + offset, 0, 0, 0))

    window = of_freq((xs, pts, recv))
    out = jax.ShapeDtypeStruct((2, 2, 2, freqs, shots, recv // 4), jnp.float32)
    out_spec = pl.BlockSpec((2, 2, 2, 1, shots, recv // 4), lambda f: (0, 0, 0, f, 0, 0))
    flops = freqs * 2 * (4 * shots) * (6 * xs * pts) * recv
    return pl.pallas_call(
        products_kernel,
        grid=(freqs,),
        in_specs=[
            pl.BlockSpec(memory_space=pltpu.SMEM),
            window,
            window,
            window,
            of_freq((xs, spread, shots), first),
            of_freq((xs, 2 * pts, shots)),
        ],
        out_specs=[out_spec, out_spec],
        out_shape=[out, out],
        compiler_params=pltpu.CompilerParams(vmem_limit_bytes=24 * 2**20),
        cost_estimate=pl.CostEstimate(
            flops=flops, bytes_accessed=freqs * 4 * 2**20, transcendentals=0
        ),
    )(place, below, here, above, own, cross)


def on_device(surface_gathers, source_gathers, aperture, live):
    pts, recv = surface_gathers.shape[3:]
    spread = source_gathers.shape[4]
    half, core = lax.axis_index("half"), lax.axis_index("core")
    place = jnp.stack([half, core]).astype(jnp.int32)
    heard = lax.broadcasted_iota(jnp.int32, surface_gathers.shape[2:], 2) < live[:, :, None]
    chunks = [(sum(CHUNKS[:i]), size) for i, size in enumerate(CHUNKS)]

    here, below, above = [], [], []
    for first, size in chunks:
        gathers = surface_gathers[:, first : first + size]
        here.append(jnp.where(heard, gathers, jnp.zeros((), gathers.dtype)))
        below.append(shifted(here[-1], 1))
        above.append(shifted(here[-1], -1))

    first_point = (2 * lax.axis_index("sup") + half) * pts - (spread - pts) // 2
    inline = first_point + lax.broadcasted_iota(jnp.int32, (spread, aperture.shape[0]), 0)
    inside = (inline >= aperture[:, 0][None, :]) & (inline < aperture[:, 1][None, :])
    shots = source_gathers.transpose(0, 1, 3, 4, 2)
    masked = jnp.where(inside, shots, jnp.zeros((), shots.dtype))
    crossing = jnp.concatenate(
        [masked[:, :, :, pts : 2 * pts], masked[:, :, :, 3 * pts : 4 * pts]], axis=3
    )
    cross = [swapped(crossing[:, first : first + size], "half") for first, size in chunks]

    predicted = []
    for i, (first, size) in enumerate(chunks):
        keep, send = products(place, below[i], here[i], above[i], masked, cross[i], first)
        partial = keep + swapped(send, "core")
        partial = partial.reshape((4,) + partial.shape[2:])
        terms = lax.all_to_all(partial, RING, 0, 0, tiled=True)
        predicted.append(terms.sum(axis=0).astype(jnp.bfloat16))
    return jnp.concatenate(predicted, axis=1)


def solution(mesh):
    fine = Mesh(
        mesh.devices.reshape(mesh.shape["shot"] // 2, 2, mesh.shape["xline"] // 2, 2),
        SHOT + XLINE,
    )
    return jax.shard_map(
        on_device,
        mesh=fine,
        in_specs=(
            P(None, None, XLINE, SHOT, None),
            P(None, None, SHOT, XLINE, None),
            P(SHOT, None),
            P(XLINE, SHOT),
        ),
        out_specs=P(None, None, SHOT, XLINE),
        check_vma=False,
    )
```

```python
import functools

import jax
import jax.numpy as jnp
from jax import lax
from jax.experimental import pallas as pl
from jax.experimental.pallas import tpu as pltpu
from jax.sharding import Mesh, PartitionSpec as P

CHUNKS = (2, 2, 2, 1, 1)
SHOT = ("sup", "half")
XLINE = ("side", "core")
RING = ("half", "side")


def shifted(block, distance):
    n = lax.axis_size("sup")
    return lax.ppermute(
        block, "sup", [(i, i + distance) for i in range(n) if 0 <= i + distance < n]
    )


def swapped(block, axis):
    return lax.ppermute(block, axis, [(0, 1), (1, 0)])


def products_kernel(place, below, here, above, own, cross, keep, send):
    half, core = place[0], place[1]
    upper = half == 1
    pts, recv = below.shape[3], below.shape[4]
    shots = own.shape[4]
    rows = below.shape[2] * pts

    def flat(values):
        return values.reshape(rows, shots)

    lefts = []
    for part in range(2):
        mine = [flat(own[part, 0, :, k * pts : (k + 1) * pts, :]) for k in range(3)]
        low, high = (flat(cross[part, 0, :, k * pts : (k + 1) * pts, :]) for k in range(2))
        none = jnp.zeros_like(low)
        theirs = [
            jnp.where(upper, low, none),
            jnp.where(upper, high, low),
            jnp.where(upper, none, high),
        ]
        lefts.append([jnp.concatenate(pair, axis=1) for pair in zip(mine, theirs)])
    total = jnp.zeros((4 * shots, recv), jnp.float32)
    for k, window in enumerate((below, here, above)):
        real, imag = lefts[0][k], lefts[1][k]
        for part, left in enumerate(
            (jnp.concatenate([real, imag], axis=1), jnp.concatenate([-imag, real], axis=1))
        ):
            total += lax.dot_general(
                left,
                window[part, 0].reshape(rows, recv),
                (((0,), (0,)), ((), ())),
                preferred_element_type=jnp.float32,
            )
    width = recv // 4
    for side in range(2):
        even = total[:, 2 * side * width : (2 * side + 1) * width]
        odd = total[:, (2 * side + 1) * width : (2 * side + 2) * width]
        stays = jnp.where(core == 0, even, odd)
        leaves = jnp.where(core == 0, odd, even)
        for part in range(2):
            for block, to in enumerate((half, 1 - half)):
                first = (2 * part + block) * shots
                keep[to, side, part, 0] = stays[first : first + shots]
                send[to, side, part, 0] = leaves[first : first + shots]


def products(place, below, here, above, own, cross):
    freqs, xs, pts, recv = here.shape[1:]
    shots = own.shape[4]

    def of_freq(shape):
        return pl.BlockSpec((2, 1) + shape, lambda f: (0, f, 0, 0, 0))

    window = of_freq((xs, pts, recv))
    out = jax.ShapeDtypeStruct((2, 2, 2, freqs, shots, recv // 4), jnp.float32)
    out_spec = pl.BlockSpec((2, 2, 2, 1, shots, recv // 4), lambda f: (0, 0, 0, f, 0, 0))
    flops = freqs * 2 * (4 * shots) * (6 * xs * pts) * recv
    return pl.pallas_call(
        products_kernel,
        grid=(freqs,),
        in_specs=[
            pl.BlockSpec(memory_space=pltpu.SMEM),
            window,
            window,
            window,
            of_freq((xs, 3 * pts, shots)),
            of_freq((xs, 2 * pts, shots)),
        ],
        out_specs=[out_spec, out_spec],
        out_shape=[out, out],
        compiler_params=pltpu.CompilerParams(vmem_limit_bytes=24 * 2**20),
        cost_estimate=pl.CostEstimate(
            flops=flops, bytes_accessed=freqs * 4 * 2**20, transcendentals=0
        ),
    )(place, below, here, above, own, cross)


def on_device(surface_gathers, source_gathers, aperture, live):
    pts, recv = surface_gathers.shape[3:]
    spread = source_gathers.shape[4]
    half, core = lax.axis_index("half"), lax.axis_index("core")
    place = jnp.stack([half, core]).astype(jnp.int32)
    heard = lax.broadcasted_iota(jnp.int32, surface_gathers.shape[2:], 2) < live[:, :, None]
    first_point = (2 * lax.axis_index("sup") + half) * pts - (spread - pts) // 2
    inline = first_point + lax.broadcasted_iota(jnp.int32, (spread, aperture.shape[0]), 0)
    inside = (inline >= aperture[:, 0][None, :]) & (inline < aperture[:, 1][None, :])
    chunks = [(sum(CHUNKS[:i]), sum(CHUNKS[: i + 1])) for i in range(len(CHUNKS))]

    def muted(gathers, i):
        gathers = gathers[:, slice(*chunks[i])]
        return jnp.where(heard, gathers, jnp.zeros((), gathers.dtype))

    def pieces(shots, i, which):
        spans = [slice(k * pts, (k + 1) * pts) for k in which]
        shots = shots[:, slice(*chunks[i])]
        return jnp.concatenate(
            [
                jnp.where(inside[span], shots[:, :, :, span], jnp.zeros((), shots.dtype))
                for span in spans
            ],
            axis=3,
        )

    shots = source_gathers.transpose(0, 1, 3, 4, 2)
    count = len(chunks)
    here, own, leaving = [None] * count, [None] * count, [None] * count
    below, above, cross = [None] * count, [None] * count, [None] * count

    def travel(i):
        below[i], above[i] = shifted(here[i], 1), shifted(here[i], -1)
        cross[i] = swapped(leaving[i], "half")

    here[0] = muted(surface_gathers, 0)
    here[0], shots, surface_gathers = lax.optimization_barrier(
        (here[0], shots, surface_gathers)
    )
    leaving[0] = pieces(shots, 0, (1, 3))
    travel(0)
    leaving[0], shots, surface_gathers = lax.optimization_barrier(
        (leaving[0], shots, surface_gathers)
    )
    for i in range(count):
        own[i] = pieces(shots, i, (0, 2, 4))
        if i:
            here[i] = muted(surface_gathers, i)
            leaving[i] = pieces(shots, i, (1, 3))
    travel(1)

    predicted = []
    for i in range(count):
        keep, send = products(place, below[i], here[i], above[i], own[i], cross[i])
        partial = keep + swapped(send, "core")
        if i + 2 < count:
            partial, own[i + 1], here[i + 2], leaving[i + 2] = lax.optimization_barrier(
                (partial, own[i + 1], here[i + 2], leaving[i + 2])
            )
            travel(i + 2)
        elif i + 1 < count:
            partial, own[i + 1] = lax.optimization_barrier((partial, own[i + 1]))
        partial = partial.reshape((4,) + partial.shape[2:])
        terms = lax.all_to_all(partial, RING, 0, 0, tiled=True)
        predicted.append((terms[0] + terms[1]) + (terms[2] + terms[3]))
    return jnp.concatenate([sums.astype(jnp.bfloat16) for sums in predicted], axis=1)


def solution(mesh):
    fine = Mesh(
        mesh.devices.reshape(mesh.shape["shot"] // 2, 2, mesh.shape["xline"] // 2, 2),
        SHOT + XLINE,
    )
    return jax.shard_map(
        on_device,
        mesh=fine,
        in_specs=(
            P(None, None, XLINE, SHOT, None),
            P(None, None, SHOT, XLINE, None),
            P(SHOT, None),
            P(XLINE, SHOT),
        ),
        out_specs=P(None, None, SHOT, XLINE),
        check_vma=False,
    )
```

```python
import functools

import jax
import jax.numpy as jnp
from jax import lax
from jax.experimental import pallas as pl
from jax.experimental.pallas import tpu as pltpu
from jax.sharding import Mesh, PartitionSpec as P

COST = 12
FIRST = 2
TOP = 32767.0
LOG = 256.0
LEAST = 2.0**-126
PAD = 16
SHOT = ("sup", "half")
XLINE = ("side", "core")
RING = ("half", "side", "core")


def shifted(block, distance):
    n = lax.axis_size("sup")
    return lax.ppermute(
        block, "sup", [(i, i + distance) for i in range(n) if 0 <= i + distance < n]
    )


def swapped(block, axes):
    n = lax.axis_size(axes)
    return lax.ppermute(block, axes, [(i, n - 1 - i) for i in range(n)])


def products_kernel(counts, place, *refs):
    out = refs[-1]
    groups, start = [], 0
    for count in counts:
        groups.append(refs[start : start + count])
        start += count
    windows, own, cross = groups[:3], groups[3], groups[4]
    half = place[0]
    upper = half == 1
    pts, recv = windows[0][0].shape[3:]
    shots = own[0].shape[4]

    def piece(blocks, part, k):
        return jnp.concatenate(
            [
                block[part, 0, :, k * pts : (k + 1) * pts, :].reshape(-1, shots)
                for block in blocks
            ],
            axis=0,
        )

    lefts, rights = [], []
    for k in range(3):
        both = []
        for part in range(2):
            low, high = piece(cross, part, 0), piece(cross, part, 1)
            none = jnp.zeros_like(low)
            theirs = (
                jnp.where(upper, low, none),
                jnp.where(upper, high, low),
                jnp.where(upper, none, high),
            )[k]
            both.append(jnp.concatenate([piece(own, part, k), theirs], axis=1))
        both = jnp.concatenate(both, axis=1).T
        real, imag = both[: 2 * shots], both[2 * shots :]
        lefts += [both, jnp.concatenate([-imag, real], axis=0)]
        rights += [
            [block[part, 0].reshape(-1, recv) for block in windows[k]] for part in range(2)
        ]
    left = jnp.concatenate(lefts, axis=1)
    right = jnp.concatenate([rows for side in rights for rows in side], axis=0)
    width = recv // 4
    total = jnp.dot(left, right, preferred_element_type=jnp.float32)
    for quarter in range(4):
        columns = total[:, quarter * width : (quarter + 1) * width]
        for block, to in enumerate((half, 1 - half)):
            values = [
                columns[(2 * part + block) * shots : (2 * part + block + 1) * shots]
                for part in range(2)
            ]
            peak = jnp.maximum(*(jnp.max(jnp.abs(v), axis=0, keepdims=True) for v in values))
            level = jnp.ceil(jnp.log2(jnp.maximum(peak, LEAST)) * LOG)
            unit = jnp.exp2(level * (-1.0 / LOG))
            for part in range(2):
                steps = jnp.clip(jnp.round(values[part] * unit * TOP), -TOP, TOP)
                out[4 * to + quarter, 0, part * shots : (part + 1) * shots] = steps.astype(
                    jnp.int32
                ).astype(jnp.int16)
            level = jnp.broadcast_to(level.astype(jnp.int32), (PAD, width))
            out[4 * to + quarter, 0, 2 * shots : 2 * shots + PAD] = level.astype(jnp.int16)


def products(place, freqs, *groups):
    arrays, starts = zip(*(block for group in groups for block in group))
    recv, shots = arrays[0].shape[4], arrays[-1].shape[4]
    rows = sum(array.shape[2] * array.shape[3] for array in arrays[: sum(map(len, groups[:3]))])
    first, count = freqs

    def spec(array, start):
        if array.shape[1] == count == 1:
            return pl.BlockSpec(memory_space=pltpu.VMEM)
        return pl.BlockSpec((2, 1) + array.shape[2:], lambda f: (0, f + first - start, 0, 0, 0))

    return pl.pallas_call(
        functools.partial(products_kernel, [len(group) for group in groups]),
        grid=(count,),
        in_specs=[pl.BlockSpec(memory_space=pltpu.SMEM)]
        + [spec(*block) for block in zip(arrays, starts)],
        out_specs=pl.BlockSpec((8, 1, 2 * shots + PAD, recv // 4), lambda f: (0, f, 0, 0)),
        out_shape=jax.ShapeDtypeStruct((8, count, 2 * shots + PAD, recv // 4), jnp.int16),
        compiler_params=pltpu.CompilerParams(vmem_limit_bytes=58 * 2**20),
        cost_estimate=pl.CostEstimate(
            flops=COST * count * 2 * (4 * shots) * (2 * rows) * recv,
            bytes_accessed=2**20,
            transcendentals=0,
        ),
        name="products",
    )(place, *arrays)


def finish_kernel(terms, *refs):
    out = refs[-1]
    shots = out.shape[3]

    def wide(values):
        return values.astype(jnp.int32).astype(jnp.float32)

    for core in range(2):
        sums = [jnp.zeros(out.shape[3:], jnp.float32) for _ in range(2)]
        for chip in range(4):
            source = 2 * chip + core
            level = wide(terms[source, 0, 2 * shots : 2 * shots + PAD])[:1]
            unit = jnp.exp2(level * (1.0 / LOG)) * (1.0 / TOP)
            for part in range(2):
                steps = wide(terms[source, 0, part * shots : (part + 1) * shots])
                sums[part] = sums[part] + steps * unit
        for part in range(2):
            out[part, core, 0] = sums[part].astype(out.dtype)


def finish(terms, freqs, count, before):
    first, size = freqs
    rows, width = terms.shape[2:]
    shots = (rows - PAD) // 2
    done = [] if before is None else [before]
    return pl.pallas_call(
        finish_kernel,
        grid=(size,),
        in_specs=[pl.BlockSpec((8, 1, rows, width), lambda f: (0, f, 0, 0))]
        + [pl.BlockSpec(memory_space=pl.ANY)] * len(done),
        out_specs=pl.BlockSpec((2, 2, 1, shots, width), lambda f: (0, 0, f + first, 0, 0)),
        out_shape=jax.ShapeDtypeStruct((2, 2, count, shots, width), jnp.bfloat16),
        input_output_aliases={1: 0} if done else {},
        compiler_params=pltpu.CompilerParams(vmem_limit_bytes=16 * 2**20),
        name="finish",
    )(terms, *done)


def on_device(surface_gathers, source_gathers, aperture, live):
    freqs_here, _, pts, recv = surface_gathers.shape[1:]
    spread = source_gathers.shape[4]
    half, core = lax.axis_index("half"), lax.axis_index("core")
    place = half.astype(jnp.int32).reshape(1)
    count = freqs_here // 2
    heard = lax.broadcasted_iota(jnp.int32, surface_gathers.shape[2:], 2) < live[:, :, None]
    first_point = (2 * lax.axis_index("sup") + half) * pts - (spread - pts) // 2
    inline = first_point + lax.broadcasted_iota(jnp.int32, (spread, aperture.shape[0]), 0)
    inside = (inline >= aperture[:, 0][None, :]) & (inline < aperture[:, 1][None, :])
    shots = source_gathers.transpose(0, 1, 3, 4, 2)

    def of_core(array, which, first, size):
        return lax.dynamic_slice_in_dim(array, which * count + first, size, 1)

    def muted(gathers, which, first, size):
        gathers = of_core(gathers, which, first, size)
        return jnp.where(heard, gathers, jnp.zeros((), gathers.dtype))

    def pieces(block, which):
        spans = [slice(k * pts, (k + 1) * pts) for k in which]
        return jnp.concatenate(
            [
                jnp.where(inside[span], block[:, :, :, span], jnp.zeros((), block.dtype))
                for span in spans
            ],
            axis=3,
        )

    early = muted(surface_gathers, core, 0, FIRST)
    early, surface_gathers, shots = lax.optimization_barrier((early, surface_gathers, shots))
    below_early, above_early = shifted(early, 1), shifted(early, -1)

    mine, others = of_core(shots, core, 0, count), of_core(shots, 1 - core, 0, count)
    cross = [
        (swapped(pieces(mine, (1, 3)), "half"), 0),
        (swapped(pieces(others, (1, 3)), ("half", "core")), 0),
    ]
    gathers = swapped(muted(surface_gathers, 1 - core, 0, count), "core")
    others = swapped(pieces(others, (0, 2, 4)), "core")
    gathers, others = lax.optimization_barrier((gathers, others))
    own = [(pieces(mine, (0, 2, 4)), 0), (others, 0)]
    early_too = gathers[:, :FIRST]
    below_too, above_too = shifted(early_too, 1), shifted(early_too, -1)
    arrived = [below_early, below_too]
    here, below, above = [], [], []
    for i in range(FIRST, count):
        block = muted(surface_gathers, core, i, 1)
        block = jnp.concatenate([block, gathers[:, i : i + 1]], axis=2)
        block, arrived[i - FIRST] = lax.optimization_barrier((block, arrived[i - FIRST]))
        here.append([(block, i)])
        below.append([(shifted(block, 1), i)])
        above.append([(shifted(block, -1), i)])
    here.insert(0, [(early, 0), (gathers, 0)])
    below.insert(0, [(block, 0) for block in arrived])
    above.insert(0, [(above_early, 0), (above_too, 0)])

    spans = [(0, FIRST)] + [(i, 1) for i in range(FIRST, count)]
    partial = [
        products(place, freqs, below[i], here[i], above[i], own, cross)
        for i, freqs in enumerate(spans)
    ]
    predicted = None
    for i, freqs in enumerate(spans):
        terms = lax.all_to_all(partial[i], RING, 0, 0, tiled=True)
        if i + 1 < len(spans):
            terms, partial[i + 1] = lax.optimization_barrier((terms, partial[i + 1]))
        predicted = finish(terms, freqs, count, predicted)
    return predicted.reshape((2, freqs_here) + predicted.shape[3:])


def solution(mesh):
    fine = Mesh(
        mesh.devices.reshape(mesh.shape["shot"] // 2, 2, mesh.shape["xline"] // 2, 2),
        SHOT + XLINE,
    )
    return jax.shard_map(
        on_device,
        mesh=fine,
        in_specs=(
            P(None, None, XLINE, SHOT, None),
            P(None, None, SHOT, XLINE, None),
            P(SHOT, None),
            P(XLINE, SHOT),
        ),
        out_specs=P(None, None, SHOT, XLINE),
        check_vma=False,
    )
```

```python
import functools

import jax
import jax.numpy as jnp
from jax import lax
from jax.experimental import pallas as pl
from jax.experimental.pallas import tpu as pltpu
from jax.sharding import Mesh, PartitionSpec as P

COST = 12
FIRST = 2
TOP = 32767.0
LOG = 256.0
LEAST = 2.0**-126
PAD = 16
STEPS = 2
SHOT = ("sup", "half")
XLINE = ("side", "core")
RING = ("half", "side", "core")


def shifted(block, distance):
    n = lax.axis_size("sup")
    return lax.ppermute(
        block, "sup", [(i, i + distance) for i in range(n) if 0 <= i + distance < n]
    )


def swapped(block, axes):
    n = lax.axis_size(axes)
    return lax.ppermute(block, axes, [(i, n - 1 - i) for i in range(n)])


def products_kernel(place, *refs):
    out, total = refs[-2:]
    windows, own, cross = (refs[0:2], refs[2:4], refs[4:6]), refs[6:8], refs[8:10]
    half = place[0]
    upper = half == 1
    pts, recv = windows[0][0].shape[3:]
    shots = own[0].shape[4]

    def piece(blocks, part, k):
        return jnp.concatenate(
            [
                block[part, 0, :, k * pts : (k + 1) * pts, :].reshape(-1, shots)
                for block in blocks
            ],
            axis=0,
        )

    lefts, rights = [], []
    for k in range(3):
        both = []
        for part in range(2):
            low, high = piece(cross, part, 0), piece(cross, part, 1)
            none = jnp.zeros_like(low)
            theirs = (
                jnp.where(upper, low, none),
                jnp.where(upper, high, low),
                jnp.where(upper, none, high),
            )[k]
            both.append(jnp.concatenate([piece(own, part, k), theirs], axis=1))
        both = jnp.concatenate(both, axis=1).T
        real, imag = both[: 2 * shots], both[2 * shots :]
        lefts += [both, jnp.concatenate([-imag, real], axis=0)]
        rights += [block[part, 0].reshape(-1, recv) for part in range(2) for block in windows[k]]
    left = jnp.concatenate(lefts, axis=1)
    right = jnp.concatenate(rights, axis=0)
    term = jnp.dot(left, right, preferred_element_type=jnp.float32)
    step, last = pl.program_id(1), pl.num_programs(1) - 1

    @pl.when(step == 0)
    def _():
        total[...] = term

    @pl.when((step > 0) & (step < last))
    def _():
        total[...] += term

    @pl.when(step == last)
    def _():
        encode(half, total[...] + term, out)


def encode(half, total, out):
    shots, width = total.shape[0] // 4, total.shape[1] // 4
    for quarter in range(4):
        columns = total[:, quarter * width : (quarter + 1) * width]
        for block, to in enumerate((half, 1 - half)):
            values = [
                columns[(2 * part + block) * shots : (2 * part + block + 1) * shots]
                for part in range(2)
            ]
            peak = jnp.maximum(*(jnp.max(jnp.abs(v), axis=0, keepdims=True) for v in values))
            level = jnp.ceil(jnp.log2(jnp.maximum(peak, LEAST)) * LOG)
            unit = jnp.exp2(level * (-1.0 / LOG))
            for part in range(2):
                steps = jnp.clip(jnp.round(values[part] * unit * TOP), -TOP, TOP)
                out[4 * to + quarter, 0, part * shots : (part + 1) * shots] = steps.astype(
                    jnp.int32
                ).astype(jnp.int16)
            level = jnp.broadcast_to(level.astype(jnp.int32), (PAD, width))
            out[4 * to + quarter, 0, 2 * shots : 2 * shots + PAD] = level.astype(jnp.int16)


def products(place, freqs, *groups):
    groups = [group if len(group) == 2 else group * 2 for group in groups]
    arrays, starts = zip(*(block for group in groups for block in group))
    recv, shots = arrays[0].shape[4], arrays[-1].shape[4]
    xs = arrays[-1].shape[2]
    rows = 6 * xs * arrays[0].shape[3]
    first, count = freqs
    step = xs // STEPS

    def spec(array, start, which):
        skip = which * STEPS if array.shape[2] > xs else 0
        return pl.BlockSpec(
            (2, 1, step) + array.shape[3:], lambda f, x: (0, f + first - start, x + skip, 0, 0)
        )

    return pl.pallas_call(
        products_kernel,
        grid=(count, STEPS),
        in_specs=[pl.BlockSpec(memory_space=pltpu.SMEM)]
        + [spec(*block, i % 2) for i, block in enumerate(zip(arrays, starts))],
        out_specs=pl.BlockSpec((8, 1, 2 * shots + PAD, recv // 4), lambda f, x: (0, f, 0, 0)),
        out_shape=jax.ShapeDtypeStruct((8, count, 2 * shots + PAD, recv // 4), jnp.int16),
        scratch_shapes=[pltpu.VMEM((4 * shots, recv), jnp.float32)],
        compiler_params=pltpu.CompilerParams(vmem_limit_bytes=58 * 2**20),
        cost_estimate=pl.CostEstimate(
            flops=COST * count * 2 * (4 * shots) * (2 * rows) * recv,
            bytes_accessed=2**20,
            transcendentals=0,
        ),
        name="products",
    )(place, *arrays)


def finish_kernel(terms, *refs):
    out = refs[-1]
    shots = out.shape[3]

    def wide(values):
        return values.astype(jnp.int32).astype(jnp.float32)

    for core in range(2):
        sums = [jnp.zeros(out.shape[3:], jnp.float32) for _ in range(2)]
        for chip in range(4):
            source = 2 * chip + core
            level = wide(terms[source, 0, 2 * shots : 2 * shots + PAD])[:1]
            unit = jnp.exp2(level * (1.0 / LOG)) * (1.0 / TOP)
            for part in range(2):
                steps = wide(terms[source, 0, part * shots : (part + 1) * shots])
                sums[part] = sums[part] + steps * unit
        for part in range(2):
            out[part, core, 0] = sums[part].astype(out.dtype)


def finish(terms, freqs, count, before):
    first, size = freqs
    rows, width = terms.shape[2:]
    shots = (rows - PAD) // 2
    done = [] if before is None else [before]
    return pl.pallas_call(
        finish_kernel,
        grid=(size,),
        in_specs=[pl.BlockSpec((8, 1, rows, width), lambda f: (0, f, 0, 0))]
        + [pl.BlockSpec(memory_space=pl.ANY)] * len(done),
        out_specs=pl.BlockSpec((2, 2, 1, shots, width), lambda f: (0, 0, f + first, 0, 0)),
        out_shape=jax.ShapeDtypeStruct((2, 2, count, shots, width), jnp.bfloat16),
        input_output_aliases={1: 0} if done else {},
        compiler_params=pltpu.CompilerParams(vmem_limit_bytes=16 * 2**20),
        name="finish",
    )(terms, *done)


def mute_kernel(place, live, mine, others, early, leaving, kept):
    step = pl.program_id(0)
    xs, pts, recv = kept.shape

    @pl.when(step == 0)
    def _():
        rows = lax.broadcasted_iota(jnp.int32, (pts, pts), 0)
        diagonal = rows == lax.broadcasted_iota(jnp.int32, (pts, pts), 1)
        receiver = lax.broadcasted_iota(jnp.int32, (pts, recv), 1).astype(jnp.float32)
        for x in range(xs):
            row = jnp.broadcast_to(live[x : x + 1, :].astype(jnp.float32), (pts, pts))
            column = jnp.sum(jnp.where(diagonal, row, 0.0), axis=1, keepdims=True)
            kept[x] = (receiver < column).astype(jnp.float32).astype(kept.dtype)
        for part in range(2):
            for freq in range(early.shape[1]):
                early[part, freq] = mine[part, freq] * kept[...]

    for part in range(2):
        for freq in range(leaving.shape[1]):
            leaving[part, freq] = others[part, freq] * kept[...]


def mute(place, gathers, live):
    freqs, xs, pts, recv = gathers.shape[1:]
    count = freqs // 2
    block = (2, FIRST, xs, pts, recv)

    def array(size):
        return jax.ShapeDtypeStruct((2, size, xs, pts, recv), gathers.dtype)

    return pl.pallas_call(
        mute_kernel,
        grid_spec=pltpu.PrefetchScalarGridSpec(
            num_scalar_prefetch=1,
            grid=(count // FIRST,),
            in_specs=[
                pl.BlockSpec((xs, pts), lambda i, place: (0, 0)),
                pl.BlockSpec(block, lambda i, place: (0, place[1] * (count // FIRST), 0, 0, 0)),
                pl.BlockSpec(
                    block, lambda i, place: (0, (1 - place[1]) * (count // FIRST) + i, 0, 0, 0)
                ),
            ],
            out_specs=[
                pl.BlockSpec(block, lambda i, place: (0, 0, 0, 0, 0)),
                pl.BlockSpec(block, lambda i, place: (0, i, 0, 0, 0)),
            ],
            scratch_shapes=[pltpu.VMEM((xs, pts, recv), gathers.dtype)],
        ),
        out_shape=[array(FIRST), array(count)],
        compiler_params=pltpu.CompilerParams(vmem_limit_bytes=58 * 2**20),
        cost_estimate=pl.CostEstimate(flops=0, bytes_accessed=6 * 2**20, transcendentals=0),
        name="mute",
    )(place, live, gathers, gathers)


def mask_kernel(plan, place, aperture, *refs):
    inside = refs[-1]
    spread, shots = inside.shape
    pts = spread // 5

    @pl.when(pl.program_id(0) == 0)
    def _():
        inline = place[2] + lax.broadcasted_iota(jnp.int32, (spread, shots), 0)
        within = (inline >= aperture[0:1, :]) & (inline < aperture[1:2, :])
        inside[...] = within.astype(jnp.float32).astype(inside.dtype)

    for source, piece, to, at, offset in plan:
        kept = inside[offset * pts : (offset + 1) * pts, :]
        for part in range(2):
            for freq in range(refs[source].shape[1]):
                refs[to][part, freq, :, at * pts : (at + 1) * pts, :] = (
                    refs[source][part, freq, :, piece * pts : (piece + 1) * pts, :] * kept
                )


def mask(place, shots, aperture, plan, sources, outputs):
    freqs, xs, spread, width = shots.shape[1:]
    count, pts = freqs // 2, spread // 5
    steps, size = count // FIRST, FIRST

    def source(other, at, pieces):
        def index(i, place):
            return (0, (place[1] ^ other) * steps + i, 0, at, 0)

        return pl.BlockSpec((2, size, xs, pieces * pts, width), index)

    moved = (sum(pieces for _, _, pieces in sources) + sum(outputs)) * 2**19
    return pl.pallas_call(
        functools.partial(mask_kernel, plan),
        grid_spec=pltpu.PrefetchScalarGridSpec(
            num_scalar_prefetch=1,
            grid=(steps,),
            in_specs=[pl.BlockSpec((2, width), lambda i, place: (0, 0))]
            + [source(*block) for block in sources],
            out_specs=[
                pl.BlockSpec((2, size, xs, pieces * pts, width), lambda i, place: (0, i, 0, 0, 0))
                for pieces in outputs
            ],
            scratch_shapes=[pltpu.VMEM((spread, width), shots.dtype)],
        ),
        out_shape=[
            jax.ShapeDtypeStruct((2, count, xs, pieces * pts, width), shots.dtype)
            for pieces in outputs
        ],
        compiler_params=pltpu.CompilerParams(vmem_limit_bytes=58 * 2**20),
        cost_estimate=pl.CostEstimate(flops=0, bytes_accessed=moved, transcendentals=0),
        name="mask",
    )(place, aperture, *[shots] * len(sources))


def on_device(surface_gathers, source_gathers, aperture, live):
    freqs_here, _, pts, _ = surface_gathers.shape[1:]
    spread = source_gathers.shape[4]
    half, core = lax.axis_index("half"), lax.axis_index("core")
    count = freqs_here // 2
    first_point = (2 * lax.axis_index("sup") + half) * pts - (spread - pts) // 2
    place = jnp.stack([half, core, first_point]).astype(jnp.int32)

    early, leaving = mute(place, surface_gathers, live)
    below_early, above_early = shifted(early, 1), shifted(early, -1)
    shots = source_gathers.transpose(0, 1, 3, 4, 2)
    crossing, cross_leaving, shots_leaving = mask(
        place,
        shots,
        aperture.T,
        ((0, 0, 3, 0, 1), (1, 0, 3, 1, 3), (2, 1, 4, 0, 1), (2, 3, 4, 1, 3))
        + tuple((2, 2 * k, 5, k, 2 * k) for k in range(3)),
        ((0, 1, 1), (0, 3, 1), (1, 0, 5)),
        (2, 2, 3),
    )
    cross = [(swapped(crossing, "half"), 0), (swapped(cross_leaving, ("half", "core")), 0)]
    gathers = swapped(leaving, "core")
    others = swapped(shots_leaving, "core")
    gathers, others, surface_gathers, shots = lax.optimization_barrier(
        (gathers, others, surface_gathers, shots)
    )
    (staying,) = mask(
        place,
        shots,
        aperture.T,
        tuple((k, 0, 3, k, 2 * k) for k in range(3)),
        ((0, 0, 1), (0, 2, 1), (0, 4, 1)),
        (3,),
    )
    heard = lax.broadcasted_iota(jnp.int32, surface_gathers.shape[2:], 2) < live[:, :, None]
    late = lax.dynamic_slice_in_dim(surface_gathers, core * count + FIRST, count - FIRST, 1)
    late = jnp.where(heard, late, jnp.zeros((), late.dtype))
    early_too = gathers[:, :FIRST]
    below_too, above_too = shifted(early_too, 1), shifted(early_too, -1)
    own = [(staying, 0), (others, 0)]
    here, below, above = [[(early, 0), (gathers, 0)]], [], []
    arrived = [below_early, above_early]
    spans = [(0, FIRST)] + [(i, 1) for i in range(FIRST, count)]
    partial = []
    for i, (first, size) in enumerate(spans):
        if i:
            block = jnp.concatenate(
                [late[:, first - FIRST : first - FIRST + 1], gathers[:, first : first + 1]], axis=2
            )
            if i == 1:
                block, arrived = lax.optimization_barrier((block, arrived))
                below.append([(arrived[0], 0), (below_too, 0)])
                above.append([(arrived[1], 0), (above_too, 0)])
                partial.append(products(place, spans[0], below[0], here[0], above[0], own, cross))
            else:
                block, partial[i - 2] = lax.optimization_barrier((block, partial[i - 2]))
            here.append([(block, first)])
            below.append([(shifted(block, 1), first)])
            above.append([(shifted(block, -1), first)])
            partial.append(products(place, spans[i], below[i], here[i], above[i], own, cross))
    predicted = None
    for i, freqs in enumerate(spans):
        terms = lax.all_to_all(partial[i], RING, 0, 0, tiled=True)
        if i + 1 < len(spans):
            terms, partial[i + 1] = lax.optimization_barrier((terms, partial[i + 1]))
        predicted = finish(terms, freqs, count, predicted)
    return predicted.reshape((2, freqs_here) + predicted.shape[3:])


def solution(mesh):
    fine = Mesh(
        mesh.devices.reshape(mesh.shape["shot"] // 2, 2, mesh.shape["xline"] // 2, 2),
        SHOT + XLINE,
    )
    return jax.shard_map(
        on_device,
        mesh=fine,
        in_specs=(
            P(None, None, XLINE, SHOT, None),
            P(None, None, SHOT, XLINE, None),
            P(SHOT, None),
            P(XLINE, SHOT),
        ),
        out_specs=P(None, None, SHOT, XLINE),
        check_vma=False,
    )
```

```python
import functools

import jax
import jax.numpy as jnp
from jax import lax
from jax.experimental import pallas as pl
from jax.experimental.pallas import tpu as pltpu
from jax.sharding import Mesh, PartitionSpec as P

COST = 12
FIRST = 2
TOP = 32767.0
LOG = 256.0
LEAST = 2.0**-126
PAD = 16
STEPS = 2
SHOT = ("sup", "half")
XLINE = ("side", "core")
RING = ("half", "side", "core")


def shifted(block, distance):
    n = lax.axis_size("sup")
    return lax.ppermute(
        block, "sup", [(i, i + distance) for i in range(n) if 0 <= i + distance < n]
    )


def swapped(block, axes):
    n = lax.axis_size(axes)
    return lax.ppermute(block, axes, [(i, n - 1 - i) for i in range(n)])


def products_kernel(place, *refs):
    out, total = refs[-2:]
    windows, own, cross = (refs[0:2], refs[2:4], refs[4:6]), refs[6:8], refs[8:10]
    half = place[0]
    upper = half == 1
    pts, recv = windows[0][0].shape[3:]
    shots = own[0].shape[4]

    def piece(blocks, part, k):
        return jnp.concatenate(
            [
                block[part, 0, :, k * pts : (k + 1) * pts, :].reshape(-1, shots)
                for block in blocks
            ],
            axis=0,
        )

    lefts, rights = [], []
    for k in range(3):
        both = []
        for part in range(2):
            low, high = piece(cross, part, 0), piece(cross, part, 1)
            none = jnp.zeros_like(low)
            theirs = (
                jnp.where(upper, low, none),
                jnp.where(upper, high, low),
                jnp.where(upper, none, high),
            )[k]
            both.append(jnp.concatenate([piece(own, part, k), theirs], axis=1))
        both = jnp.concatenate(both, axis=1).T
        real, imag = both[: 2 * shots], both[2 * shots :]
        lefts += [both, jnp.concatenate([-imag, real], axis=0)]
        rights += [block[part, 0].reshape(-1, recv) for part in range(2) for block in windows[k]]
    left = jnp.concatenate(lefts, axis=1)
    right = jnp.concatenate(rights, axis=0)
    term = jnp.dot(left, right, preferred_element_type=jnp.float32)
    step, last = pl.program_id(1), pl.num_programs(1) - 1

    @pl.when(step == 0)
    def _():
        total[...] = term

    @pl.when((step > 0) & (step < last))
    def _():
        total[...] += term

    @pl.when(step == last)
    def _():
        encode(half, total[...] + term, out)


def encode(half, total, out):
    shots, width = total.shape[0] // 4, total.shape[1] // 4
    for quarter in range(4):
        columns = total[:, quarter * width : (quarter + 1) * width]
        for block, to in enumerate((half, 1 - half)):
            values = [
                columns[(2 * part + block) * shots : (2 * part + block + 1) * shots]
                for part in range(2)
            ]
            peak = jnp.maximum(*(jnp.max(jnp.abs(v), axis=0, keepdims=True) for v in values))
            level = jnp.ceil(jnp.log2(jnp.maximum(peak, LEAST)) * LOG)
            unit = jnp.exp2(level * (-1.0 / LOG))
            for part in range(2):
                steps = jnp.clip(jnp.round(values[part] * unit * TOP), -TOP, TOP)
                out[4 * to + quarter, 0, part * shots : (part + 1) * shots] = steps.astype(
                    jnp.int32
                ).astype(jnp.int16)
            level = jnp.broadcast_to(level.astype(jnp.int32), (PAD, width))
            out[4 * to + quarter, 0, 2 * shots : 2 * shots + PAD] = level.astype(jnp.int16)


def products(place, freqs, *groups):
    groups = [group if len(group) == 2 else group * 2 for group in groups]
    arrays, starts = zip(*(block for group in groups for block in group))
    recv, shots = arrays[0].shape[4], arrays[-1].shape[4]
    xs = arrays[-1].shape[2]
    rows = 6 * xs * arrays[0].shape[3]
    first, count = freqs
    step = xs // STEPS

    def spec(array, start, which):
        skip = which * STEPS if array.shape[2] > xs else 0
        return pl.BlockSpec(
            (2, 1, step) + array.shape[3:], lambda f, x: (0, f + first - start, x + skip, 0, 0)
        )

    return pl.pallas_call(
        products_kernel,
        grid=(count, STEPS),
        in_specs=[pl.BlockSpec(memory_space=pltpu.SMEM)]
        + [spec(*block, i % 2) for i, block in enumerate(zip(arrays, starts))],
        out_specs=pl.BlockSpec((8, 1, 2 * shots + PAD, recv // 4), lambda f, x: (0, f, 0, 0)),
        out_shape=jax.ShapeDtypeStruct((8, count, 2 * shots + PAD, recv // 4), jnp.int16),
        scratch_shapes=[pltpu.VMEM((4 * shots, recv), jnp.float32)],
        compiler_params=pltpu.CompilerParams(vmem_limit_bytes=58 * 2**20),
        cost_estimate=pl.CostEstimate(
            flops=COST * count * 2 * (4 * shots) * (2 * rows) * recv,
            bytes_accessed=2**20,
            transcendentals=0,
        ),
        name="products",
    )(place, *arrays)


def finish_kernel(terms, *refs):
    out = refs[-1]
    shots = out.shape[3]

    def wide(values):
        return values.astype(jnp.int32).astype(jnp.float32)

    for core in range(2):
        sums = [jnp.zeros(out.shape[3:], jnp.float32) for _ in range(2)]
        for chip in range(4):
            source = 2 * chip + core
            level = wide(terms[source, 0, 2 * shots : 2 * shots + PAD])[:1]
            unit = jnp.exp2(level * (1.0 / LOG)) * (1.0 / TOP)
            for part in range(2):
                steps = wide(terms[source, 0, part * shots : (part + 1) * shots])
                sums[part] = sums[part] + steps * unit
        for part in range(2):
            out[part, core, 0] = sums[part].astype(out.dtype)


def finish(terms, freqs, count, before):
    first, size = freqs
    rows, width = terms.shape[2:]
    shots = (rows - PAD) // 2
    done = [] if before is None else [before]
    return pl.pallas_call(
        finish_kernel,
        grid=(size,),
        in_specs=[pl.BlockSpec((8, 1, rows, width), lambda f: (0, f, 0, 0))]
        + [pl.BlockSpec(memory_space=pl.ANY)] * len(done),
        out_specs=pl.BlockSpec((2, 2, 1, shots, width), lambda f: (0, 0, f + first, 0, 0)),
        out_shape=jax.ShapeDtypeStruct((2, 2, count, shots, width), jnp.bfloat16),
        input_output_aliases={1: 0} if done else {},
        compiler_params=pltpu.CompilerParams(vmem_limit_bytes=16 * 2**20),
        name="finish",
    )(terms, *done)


def keep_live(live, kept):
    xs, pts, recv = kept.shape
    rows = lax.broadcasted_iota(jnp.int32, (pts, pts), 0)
    diagonal = rows == lax.broadcasted_iota(jnp.int32, (pts, pts), 1)
    receiver = lax.broadcasted_iota(jnp.int32, (pts, recv), 1).astype(jnp.float32)
    for x in range(xs):
        row = jnp.broadcast_to(live[x : x + 1, :].astype(jnp.float32), (pts, pts))
        column = jnp.sum(jnp.where(diagonal, row, 0.0), axis=1, keepdims=True)
        kept[x] = (receiver < column).astype(jnp.float32).astype(kept.dtype)


def keep_inside(first_point, aperture, inside):
    inline = first_point + lax.broadcasted_iota(jnp.int32, inside.shape, 0)
    within = (inline >= aperture[0:1, :]) & (inline < aperture[1:2, :])
    inside[...] = within.astype(jnp.float32).astype(inside.dtype)


def put_masked(source, piece, to, at, offset, inside):
    pts = inside.shape[0] // 5
    kept = inside[offset * pts : (offset + 1) * pts, :]
    for part in range(2):
        for freq in range(source.shape[1]):
            to[part, freq, :, at * pts : (at + 1) * pts, :] = (
                source[part, freq, :, piece * pts : (piece + 1) * pts, :] * kept
            )


def first_kernel(place, live, aperture, *refs):
    mine, others, low, high, other_shots = refs[:5]
    early, leaving, crossing, cross_leaving, shots_leaving, kept, inside = refs[5:]

    @pl.when(pl.program_id(0) == 0)
    def _():
        keep_live(live, kept)
        keep_inside(place[2], aperture, inside)
        for part in range(2):
            for freq in range(early.shape[1]):
                early[part, freq] = mine[part, freq] * kept[...]

    for part in range(2):
        for freq in range(leaving.shape[1]):
            leaving[part, freq] = others[part, freq] * kept[...]
    put_masked(low, 0, crossing, 0, 1, inside)
    put_masked(high, 0, crossing, 1, 3, inside)
    for k in range(5):
        put_masked(other_shots, k, cross_leaving if k % 2 else shots_leaving, k // 2, k, inside)


def second_kernel(place, aperture, below, here, above, staying, inside):
    @pl.when(pl.program_id(0) == 0)
    def _():
        keep_inside(place[2], aperture, inside)

    for k, source in enumerate((below, here, above)):
        put_masked(source, 0, staying, k, 2 * k, inside)


def prepare(place, gathers, live, shots, aperture):
    freqs, xs, pts, recv = gathers.shape[1:]
    spread, width = shots.shape[3:]
    count = freqs // 2
    steps = count // FIRST

    def block(rows, columns):
        return (2, FIRST, xs, rows, columns)

    def source(other, at, rows):
        def index(i, place):
            return (0, (place[1] ^ other) * steps + i, 0, at, 0)

        return pl.BlockSpec(block(rows, width), index)

    def result(rows, columns):
        return pl.BlockSpec(block(rows, columns), lambda i, place: (0, i, 0, 0, 0))

    sizes = (2 * pts, 2 * pts, 3 * pts)
    return pl.pallas_call(
        first_kernel,
        grid_spec=pltpu.PrefetchScalarGridSpec(
            num_scalar_prefetch=1,
            grid=(steps,),
            in_specs=[
                pl.BlockSpec((xs, pts), lambda i, place: (0, 0)),
                pl.BlockSpec((2, width), lambda i, place: (0, 0)),
                pl.BlockSpec(block(pts, recv), lambda i, place: (0, place[1] * steps, 0, 0, 0)),
                pl.BlockSpec(
                    block(pts, recv), lambda i, place: (0, (1 - place[1]) * steps + i, 0, 0, 0)
                ),
                source(0, 1, pts),
                source(0, 3, pts),
                source(1, 0, spread),
            ],
            out_specs=[
                pl.BlockSpec(block(pts, recv), lambda i, place: (0, 0, 0, 0, 0)),
                result(pts, recv),
            ]
            + [result(rows, width) for rows in sizes],
            scratch_shapes=[
                pltpu.VMEM((xs, pts, recv), gathers.dtype),
                pltpu.VMEM((spread, width), shots.dtype),
            ],
        ),
        out_shape=[
            jax.ShapeDtypeStruct((2, FIRST, xs, pts, recv), gathers.dtype),
            jax.ShapeDtypeStruct((2, count, xs, pts, recv), gathers.dtype),
        ]
        + [jax.ShapeDtypeStruct((2, count, xs, rows, width), shots.dtype) for rows in sizes],
        compiler_params=pltpu.CompilerParams(vmem_limit_bytes=58 * 2**20),
        cost_estimate=pl.CostEstimate(flops=0, bytes_accessed=13 * 2**20, transcendentals=0),
        name="prepare",
    )(place, live, aperture, gathers, gathers, shots, shots, shots)


def stay(place, shots, aperture):
    freqs, xs, spread, width = shots.shape[1:]
    count, pts = freqs // 2, spread // 5
    steps = count // FIRST

    def source(at):
        return pl.BlockSpec(
            (2, FIRST, xs, pts, width), lambda i, place: (0, place[1] * steps + i, 0, at, 0)
        )

    return pl.pallas_call(
        second_kernel,
        grid_spec=pltpu.PrefetchScalarGridSpec(
            num_scalar_prefetch=1,
            grid=(steps,),
            in_specs=[pl.BlockSpec((2, width), lambda i, place: (0, 0))]
            + [source(at) for at in (0, 2, 4)],
            out_specs=pl.BlockSpec(
                (2, FIRST, xs, 3 * pts, width), lambda i, place: (0, i, 0, 0, 0)
            ),
            scratch_shapes=[pltpu.VMEM((spread, width), shots.dtype)],
        ),
        out_shape=jax.ShapeDtypeStruct((2, count, xs, 3 * pts, width), shots.dtype),
        compiler_params=pltpu.CompilerParams(vmem_limit_bytes=58 * 2**20),
        cost_estimate=pl.CostEstimate(flops=0, bytes_accessed=3 * 2**20, transcendentals=0),
        name="stay",
    )(place, aperture, shots, shots, shots)


def on_device(surface_gathers, source_gathers, aperture, live):
    freqs_here, _, pts, _ = surface_gathers.shape[1:]
    spread = source_gathers.shape[4]
    half, core = lax.axis_index("half"), lax.axis_index("core")
    count = freqs_here // 2
    first_point = (2 * lax.axis_index("sup") + half) * pts - (spread - pts) // 2
    place = jnp.stack([half, core, first_point]).astype(jnp.int32)

    shots = source_gathers.transpose(0, 1, 3, 4, 2)
    early, leaving, crossing, cross_leaving, shots_leaving = prepare(
        place, surface_gathers, live, shots, aperture.T
    )
    below_early, above_early = shifted(early, 1), shifted(early, -1)
    gathers = swapped(leaving, "core")
    others = swapped(shots_leaving, "core")
    cross = [(swapped(crossing, "half"), 0), (swapped(cross_leaving, ("half", "core")), 0)]
    gathers, surface_gathers = lax.optimization_barrier((gathers, surface_gathers))
    others, shots = lax.optimization_barrier((others, shots))
    staying = stay(place, shots, aperture.T)
    heard = lax.broadcasted_iota(jnp.int32, surface_gathers.shape[2:], 2) < live[:, :, None]
    late = lax.dynamic_slice_in_dim(surface_gathers, core * count + FIRST, count - FIRST, 1)
    late = jnp.where(heard, late, jnp.zeros((), late.dtype))
    early_too = gathers[:, :FIRST]
    below_too, above_too = shifted(early_too, 1), shifted(early_too, -1)
    own = [(staying, 0), (others, 0)]
    here, below, above = [[(early, 0), (gathers, 0)]], [], []
    arrived = [below_early, above_early]
    spans = [(0, FIRST)] + [(i, 1) for i in range(FIRST, count)]
    for i, (first, size) in enumerate(spans):
        if i:
            block = jnp.concatenate(
                [late[:, first - FIRST : first - FIRST + 1], gathers[:, first : first + 1]], axis=2
            )
            if i == 1:
                block, arrived = lax.optimization_barrier((block, arrived))
                block_after = [below_too, above_too]
            else:
                block, block_after = lax.optimization_barrier((block, block_after))
                below.insert(0, [(arrived[0], 0), (block_after[0], 0)])
                above.insert(0, [(arrived[1], 0), (block_after[1], 0)])
            here.append([(block, first)])
            below.append([(shifted(block, 1), first)])
            above.append([(shifted(block, -1), first)])
    partial = [
        products(place, spans[i], below[i], here[i], above[i], own, cross)
        for i in range(len(spans))
    ]
    predicted = None
    for i, freqs in enumerate(spans):
        terms = lax.all_to_all(partial[i], RING, 0, 0, tiled=True)
        if i + 1 < len(spans):
            terms, partial[i + 1] = lax.optimization_barrier((terms, partial[i + 1]))
        predicted = finish(terms, freqs, count, predicted)
    return predicted.reshape((2, freqs_here) + predicted.shape[3:])


def solution(mesh):
    fine = Mesh(
        mesh.devices.reshape(mesh.shape["shot"] // 2, 2, mesh.shape["xline"] // 2, 2),
        SHOT + XLINE,
    )
    return jax.shard_map(
        on_device,
        mesh=fine,
        in_specs=(
            P(None, None, XLINE, SHOT, None),
            P(None, None, SHOT, XLINE, None),
            P(SHOT, None),
            P(XLINE, SHOT),
        ),
        out_specs=P(None, None, SHOT, XLINE),
        check_vma=False,
    )
```

```python
import functools

import jax
import jax.numpy as jnp
from jax import lax
from jax.experimental import pallas as pl
from jax.experimental.pallas import tpu as pltpu
from jax.sharding import Mesh, PartitionSpec as P

COST = 12
FIRST = 2
TOP = 32767.0
LOG = 256.0
LEAST = 2.0**-126
PAD = 16
STEPS = 2
SHOT = ("sup", "half")
XLINE = ("side", "core")
RING = ("half", "side", "core")


def shifted(block, distance):
    n = lax.axis_size("sup")
    return lax.ppermute(
        block, "sup", [(i, i + distance) for i in range(n) if 0 <= i + distance < n]
    )


def swapped(block, axes):
    n = lax.axis_size(axes)
    return lax.ppermute(block, axes, [(i, n - 1 - i) for i in range(n)])


def products_kernel(place, *refs):
    out, total = refs[-2:]
    windows, own, cross = (refs[0:2], refs[2:4], refs[4:6]), refs[6:8], refs[8:10]
    half = place[0]
    upper = half == 1
    pts, recv = windows[0][0].shape[3:]
    shots = own[0].shape[4]

    def piece(blocks, part, k):
        return jnp.concatenate(
            [
                block[part, 0, :, k * pts : (k + 1) * pts, :].reshape(-1, shots)
                for block in blocks
            ],
            axis=0,
        )

    lefts, rights = [], []
    for k in range(3):
        both = []
        for part in range(2):
            low, high = piece(cross, part, 0), piece(cross, part, 1)
            none = jnp.zeros_like(low)
            theirs = (
                jnp.where(upper, low, none),
                jnp.where(upper, high, low),
                jnp.where(upper, none, high),
            )[k]
            both.append(jnp.concatenate([piece(own, part, k), theirs], axis=1))
        both = jnp.concatenate(both, axis=1).T
        real, imag = both[: 2 * shots], both[2 * shots :]
        lefts += [both, jnp.concatenate([-imag, real], axis=0)]
        rights += [block[part, 0].reshape(-1, recv) for part in range(2) for block in windows[k]]
    left = jnp.concatenate(lefts, axis=1)
    right = jnp.concatenate(rights, axis=0)
    term = jnp.dot(left, right, preferred_element_type=jnp.float32)
    step, last = pl.program_id(1), pl.num_programs(1) - 1

    @pl.when(step == 0)
    def _():
        total[...] = term

    @pl.when((step > 0) & (step < last))
    def _():
        total[...] += term

    @pl.when(step == last)
    def _():
        encode(half, total[...] + term, out)


def encode(half, total, out):
    shots, width = total.shape[0] // 4, total.shape[1] // 4
    for quarter in range(4):
        columns = total[:, quarter * width : (quarter + 1) * width]
        for block, to in enumerate((half, 1 - half)):
            values = [
                columns[(2 * part + block) * shots : (2 * part + block + 1) * shots]
                for part in range(2)
            ]
            peak = jnp.maximum(*(jnp.max(jnp.abs(v), axis=0, keepdims=True) for v in values))
            level = jnp.ceil(jnp.log2(jnp.maximum(peak, LEAST)) * LOG)
            unit = jnp.exp2(level * (-1.0 / LOG))
            for part in range(2):
                steps = jnp.clip(jnp.round(values[part] * unit * TOP), -TOP, TOP)
                out[4 * to + quarter, 0, part * shots : (part + 1) * shots] = steps.astype(
                    jnp.int32
                ).astype(jnp.int16)
            level = jnp.broadcast_to(level.astype(jnp.int32), (PAD, width))
            out[4 * to + quarter, 0, 2 * shots : 2 * shots + PAD] = level.astype(jnp.int16)


def products(place, freqs, *groups):
    groups = [group if len(group) == 2 else group * 2 for group in groups]
    arrays, starts = zip(*(block for group in groups for block in group))
    recv, shots = arrays[0].shape[4], arrays[-1].shape[4]
    xs = arrays[-1].shape[2]
    rows = 6 * xs * arrays[0].shape[3]
    first, count = freqs
    step = xs // STEPS

    def spec(array, start, which):
        skip = which * STEPS if array.shape[2] > xs else 0
        return pl.BlockSpec(
            (2, 1, step) + array.shape[3:], lambda f, x: (0, f + first - start, x + skip, 0, 0)
        )

    return pl.pallas_call(
        products_kernel,
        grid=(count, STEPS),
        in_specs=[pl.BlockSpec(memory_space=pltpu.SMEM)]
        + [spec(*block, i % 2) for i, block in enumerate(zip(arrays, starts))],
        out_specs=pl.BlockSpec((8, 1, 2 * shots + PAD, recv // 4), lambda f, x: (0, f, 0, 0)),
        out_shape=jax.ShapeDtypeStruct((8, count, 2 * shots + PAD, recv // 4), jnp.int16),
        scratch_shapes=[pltpu.VMEM((4 * shots, recv), jnp.float32)],
        compiler_params=pltpu.CompilerParams(vmem_limit_bytes=58 * 2**20),
        cost_estimate=pl.CostEstimate(
            flops=COST * count * 2 * (4 * shots) * (2 * rows) * recv,
            bytes_accessed=2**20,
            transcendentals=0,
        ),
        name="products",
    )(place, *arrays)


def finish_kernel(terms, *refs):
    out = refs[-1]
    shots = out.shape[3]

    def wide(values):
        return values.astype(jnp.int32).astype(jnp.float32)

    for core in range(2):
        sums = [jnp.zeros(out.shape[3:], jnp.float32) for _ in range(2)]
        for chip in range(4):
            source = 2 * chip + core
            level = wide(terms[source, 0, 2 * shots : 2 * shots + PAD])[:1]
            unit = jnp.exp2(level * (1.0 / LOG)) * (1.0 / TOP)
            for part in range(2):
                steps = wide(terms[source, 0, part * shots : (part + 1) * shots])
                sums[part] = sums[part] + steps * unit
        for part in range(2):
            out[part, core, 0] = sums[part].astype(out.dtype)


def finish(terms, freqs, count, before):
    first, size = freqs
    rows, width = terms.shape[2:]
    shots = (rows - PAD) // 2
    done = [] if before is None else [before]
    return pl.pallas_call(
        finish_kernel,
        grid=(size,),
        in_specs=[pl.BlockSpec((8, 1, rows, width), lambda f: (0, f, 0, 0))]
        + [pl.BlockSpec(memory_space=pl.ANY)] * len(done),
        out_specs=pl.BlockSpec((2, 2, 1, shots, width), lambda f: (0, 0, f + first, 0, 0)),
        out_shape=jax.ShapeDtypeStruct((2, 2, count, shots, width), jnp.bfloat16),
        input_output_aliases={1: 0} if done else {},
        compiler_params=pltpu.CompilerParams(vmem_limit_bytes=16 * 2**20),
        name="finish",
    )(terms, *done)


def keep_live(live, kept):
    xs, pts, recv = kept.shape
    rows = lax.broadcasted_iota(jnp.int32, (pts, pts), 0)
    diagonal = rows == lax.broadcasted_iota(jnp.int32, (pts, pts), 1)
    receiver = lax.broadcasted_iota(jnp.int32, (pts, recv), 1).astype(jnp.float32)
    for x in range(xs):
        row = jnp.broadcast_to(live[x : x + 1, :].astype(jnp.float32), (pts, pts))
        column = jnp.sum(jnp.where(diagonal, row, 0.0), axis=1, keepdims=True)
        kept[x] = (receiver < column).astype(jnp.float32).astype(kept.dtype)


def keep_inside(first_point, aperture, inside):
    inline = first_point + lax.broadcasted_iota(jnp.int32, inside.shape, 0)
    within = (inline >= aperture[0:1, :]) & (inline < aperture[1:2, :])
    inside[...] = within.astype(jnp.float32).astype(inside.dtype)


def put_masked(source, piece, to, at, offset, inside):
    pts = inside.shape[0] // 5
    kept = inside[offset * pts : (offset + 1) * pts, :]
    for part in range(2):
        for freq in range(source.shape[1]):
            to[part, freq, :, at * pts : (at + 1) * pts, :] = (
                source[part, freq, :, piece * pts : (piece + 1) * pts, :] * kept
            )


def first_kernel(place, live, aperture, *refs):
    mine, others, low, high, other_shots = refs[:5]
    early, leaving, crossing, cross_leaving, shots_leaving, kept, inside = refs[5:]

    @pl.when(pl.program_id(0) == 0)
    def _():
        keep_live(live, kept)
        keep_inside(place[2], aperture, inside)
        for part in range(2):
            for freq in range(early.shape[1]):
                early[part, freq] = mine[part, freq] * kept[...]

    for part in range(2):
        for freq in range(leaving.shape[1]):
            leaving[part, freq] = others[part, freq] * kept[...]
    put_masked(low, 0, crossing, 0, 1, inside)
    put_masked(high, 0, crossing, 1, 3, inside)
    for k in range(5):
        put_masked(other_shots, k, cross_leaving if k % 2 else shots_leaving, k // 2, k, inside)


def second_kernel(place, aperture, below, here, above, staying, inside):
    @pl.when(pl.program_id(0) == 0)
    def _():
        keep_inside(place[2], aperture, inside)

    for k, source in enumerate((below, here, above)):
        put_masked(source, 0, staying, k, 2 * k, inside)


def prepare(place, gathers, live, shots, aperture):
    freqs, xs, pts, recv = gathers.shape[1:]
    spread, width = shots.shape[3:]
    count = freqs // 2
    steps = count // FIRST

    def block(rows, columns):
        return (2, FIRST, xs, rows, columns)

    def source(other, at, rows):
        def index(i, place):
            return (0, (place[1] ^ other) * steps + i, 0, at, 0)

        return pl.BlockSpec(block(rows, width), index)

    def result(rows, columns):
        return pl.BlockSpec(block(rows, columns), lambda i, place: (0, i, 0, 0, 0))

    sizes = (2 * pts, 2 * pts, 3 * pts)
    return pl.pallas_call(
        first_kernel,
        grid_spec=pltpu.PrefetchScalarGridSpec(
            num_scalar_prefetch=1,
            grid=(steps,),
            in_specs=[
                pl.BlockSpec((xs, pts), lambda i, place: (0, 0)),
                pl.BlockSpec((2, width), lambda i, place: (0, 0)),
                pl.BlockSpec(block(pts, recv), lambda i, place: (0, place[1] * steps, 0, 0, 0)),
                pl.BlockSpec(
                    block(pts, recv), lambda i, place: (0, (1 - place[1]) * steps + i, 0, 0, 0)
                ),
                source(0, 1, pts),
                source(0, 3, pts),
                source(1, 0, spread),
            ],
            out_specs=[
                pl.BlockSpec(block(pts, recv), lambda i, place: (0, 0, 0, 0, 0)),
                result(pts, recv),
            ]
            + [result(rows, width) for rows in sizes],
            scratch_shapes=[
                pltpu.VMEM((xs, pts, recv), gathers.dtype),
                pltpu.VMEM((spread, width), shots.dtype),
            ],
        ),
        out_shape=[
            jax.ShapeDtypeStruct((2, FIRST, xs, pts, recv), gathers.dtype),
            jax.ShapeDtypeStruct((2, count, xs, pts, recv), gathers.dtype),
        ]
        + [jax.ShapeDtypeStruct((2, count, xs, rows, width), shots.dtype) for rows in sizes],
        compiler_params=pltpu.CompilerParams(vmem_limit_bytes=58 * 2**20),
        cost_estimate=pl.CostEstimate(flops=0, bytes_accessed=13 * 2**20, transcendentals=0),
        name="prepare",
    )(place, live, aperture, gathers, gathers, shots, shots, shots)


def stay(place, shots, aperture):
    freqs, xs, spread, width = shots.shape[1:]
    count, pts = freqs // 2, spread // 5
    steps = count // FIRST

    def source(at):
        return pl.BlockSpec(
            (2, FIRST, xs, pts, width), lambda i, place: (0, place[1] * steps + i, 0, at, 0)
        )

    return pl.pallas_call(
        second_kernel,
        grid_spec=pltpu.PrefetchScalarGridSpec(
            num_scalar_prefetch=1,
            grid=(steps,),
            in_specs=[pl.BlockSpec((2, width), lambda i, place: (0, 0))]
            + [source(at) for at in (0, 2, 4)],
            out_specs=pl.BlockSpec(
                (2, FIRST, xs, 3 * pts, width), lambda i, place: (0, i, 0, 0, 0)
            ),
            scratch_shapes=[pltpu.VMEM((spread, width), shots.dtype)],
        ),
        out_shape=jax.ShapeDtypeStruct((2, count, xs, 3 * pts, width), shots.dtype),
        compiler_params=pltpu.CompilerParams(vmem_limit_bytes=58 * 2**20),
        cost_estimate=pl.CostEstimate(flops=0, bytes_accessed=3 * 2**20, transcendentals=0),
        name="stay",
    )(place, aperture, shots, shots, shots)


def on_device(surface_gathers, source_gathers, aperture, live):
    freqs_here, _, pts, _ = surface_gathers.shape[1:]
    spread = source_gathers.shape[4]
    half, core = lax.axis_index("half"), lax.axis_index("core")
    count = freqs_here // 2
    first_point = (2 * lax.axis_index("sup") + half) * pts - (spread - pts) // 2
    place = jnp.stack([half, core, first_point]).astype(jnp.int32)

    shots = source_gathers.transpose(0, 1, 3, 4, 2)
    early, leaving, crossing, cross_leaving, shots_leaving = prepare(
        place, surface_gathers, live, shots, aperture.T
    )
    below_early, above_early = shifted(early, 1), shifted(early, -1)
    gathers = swapped(leaving, "core")
    others = swapped(shots_leaving, "core")
    cross = [(swapped(crossing, "half"), 0), (swapped(cross_leaving, ("half", "core")), 0)]
    gathers, surface_gathers = lax.optimization_barrier((gathers, surface_gathers))
    others, shots = lax.optimization_barrier((others, shots))
    staying = stay(place, shots, aperture.T)
    heard = lax.broadcasted_iota(jnp.int32, surface_gathers.shape[2:], 2) < live[:, :, None]
    late = lax.dynamic_slice_in_dim(surface_gathers, core * count + FIRST, count - FIRST, 1)
    late = jnp.where(heard, late, jnp.zeros((), late.dtype))
    early_too = gathers[:, :FIRST]
    below_too, above_too = shifted(early_too, 1), shifted(early_too, -1)
    own = [(staying, 0), (others, 0)]
    here, below, above = [[(early, 0), (gathers, 0)]], [], []
    arrived = [below_early, above_early]
    spans = [(0, FIRST)] + [(i, 1) for i in range(FIRST, count)]
    for i, (first, size) in enumerate(spans):
        if i:
            block = jnp.concatenate(
                [late[:, first - FIRST : first - FIRST + 1], gathers[:, first : first + 1]], axis=2
            )
            if i == 1:
                block, arrived = lax.optimization_barrier((block, arrived))
                block_after = [below_too, above_too]
            else:
                block, block_after[0] = lax.optimization_barrier((block, block_after[0]))
                below.insert(0, [(arrived[0], 0), (block_after[0], 0)])
                above.insert(0, [(arrived[1], 0), (block_after[1], 0)])
            here.append([(block, first)])
            below.append([(shifted(block, 1), first)])
            above.append([(shifted(block, -1), first)])
    partial = [
        products(place, spans[i], below[i], here[i], above[i], own, cross)
        for i in range(len(spans))
    ]
    predicted = None
    for i, freqs in enumerate(spans):
        terms = lax.all_to_all(partial[i], RING, 0, 0, tiled=True)
        if i + 1 < len(spans):
            terms, partial[i + 1] = lax.optimization_barrier((terms, partial[i + 1]))
        predicted = finish(terms, freqs, count, predicted)
    return predicted.reshape((2, freqs_here) + predicted.shape[3:])


def solution(mesh):
    fine = Mesh(
        mesh.devices.reshape(mesh.shape["shot"] // 2, 2, mesh.shape["xline"] // 2, 2),
        SHOT + XLINE,
    )
    return jax.shard_map(
        on_device,
        mesh=fine,
        in_specs=(
            P(None, None, XLINE, SHOT, None),
            P(None, None, SHOT, XLINE, None),
            P(SHOT, None),
            P(XLINE, SHOT),
        ),
        out_specs=P(None, None, SHOT, XLINE),
        check_vma=False,
    )
```

```python
import functools

import jax
import jax.numpy as jnp
from jax import lax
from jax.experimental import pallas as pl
from jax.experimental.pallas import tpu as pltpu
from jax.sharding import Mesh, PartitionSpec as P

COST = 12
FIRST = 2
TOP = 32767.0
LOG = 256.0
LEAST = 2.0**-126
PAD = 16
STEPS = 2
SHOT = ("sup", "half")
XLINE = ("side", "core")
RING = ("half", "side", "core")


def shifted(block, distance):
    n = lax.axis_size("sup")
    return lax.ppermute(
        block, "sup", [(i, i + distance) for i in range(n) if 0 <= i + distance < n]
    )


def swapped(block, axes):
    n = lax.axis_size(axes)
    return lax.ppermute(block, axes, [(i, n - 1 - i) for i in range(n)])


def core_of(place):
    return place[0] & 1


def half_of(place):
    return (place[0] >> 2) & 1


def first_of(place, pts):
    return (place[0] >> 2) * pts - 2 * pts


def products_kernel(place, *refs):
    out, total = refs[-2:]
    windows, own, cross = (refs[0:2], refs[2:4], refs[4:6]), refs[6:8], refs[8:10]
    half = half_of(place)
    upper = half == 1
    pts, recv = windows[0][0].shape[3:]
    shots = own[0].shape[4]

    def piece(blocks, part, k):
        return jnp.concatenate(
            [
                block[part, 0, :, k * pts : (k + 1) * pts, :].reshape(-1, shots)
                for block in blocks
            ],
            axis=0,
        )

    lefts, rights = [], []
    for k in range(3):
        both = []
        for part in range(2):
            low, high = piece(cross, part, 0), piece(cross, part, 1)
            none = jnp.zeros_like(low)
            theirs = (
                jnp.where(upper, low, none),
                jnp.where(upper, high, low),
                jnp.where(upper, none, high),
            )[k]
            both.append(jnp.concatenate([piece(own, part, k), theirs], axis=1))
        both = jnp.concatenate(both, axis=1).T
        real, imag = both[: 2 * shots], both[2 * shots :]
        lefts += [both, jnp.concatenate([-imag, real], axis=0)]
        rights += [block[part, 0].reshape(-1, recv) for part in range(2) for block in windows[k]]
    left = jnp.concatenate(lefts, axis=1)
    right = jnp.concatenate(rights, axis=0)
    term = jnp.dot(left, right, preferred_element_type=jnp.float32)
    step, last = pl.program_id(1), pl.num_programs(1) - 1

    @pl.when(step == 0)
    def _():
        total[...] = term

    @pl.when((step > 0) & (step < last))
    def _():
        total[...] += term

    @pl.when(step == last)
    def _():
        encode(half, total[...] + term, out)


def encode(half, total, out):
    shots, width = total.shape[0] // 4, total.shape[1] // 4
    for quarter in range(4):
        columns = total[:, quarter * width : (quarter + 1) * width]
        for block, to in enumerate((half, 1 - half)):
            values = [
                columns[(2 * part + block) * shots : (2 * part + block + 1) * shots]
                for part in range(2)
            ]
            peak = jnp.maximum(*(jnp.max(jnp.abs(v), axis=0, keepdims=True) for v in values))
            level = jnp.ceil(jnp.log2(jnp.maximum(peak, LEAST)) * LOG)
            unit = jnp.exp2(level * (-1.0 / LOG))
            for part in range(2):
                steps = jnp.clip(jnp.round(values[part] * unit * TOP), -TOP, TOP)
                out[4 * to + quarter, 0, part * shots : (part + 1) * shots] = steps.astype(
                    jnp.int32
                ).astype(jnp.int16)
            level = jnp.broadcast_to(level.astype(jnp.int32), (PAD, width))
            out[4 * to + quarter, 0, 2 * shots : 2 * shots + PAD] = level.astype(jnp.int16)


def products(place, freqs, *groups):
    groups = [group if len(group) == 2 else group * 2 for group in groups]
    arrays, starts = zip(*(block for group in groups for block in group))
    recv, shots = arrays[0].shape[4], arrays[-1].shape[4]
    xs = arrays[-1].shape[2]
    rows = 6 * xs * arrays[0].shape[3]
    first, count = freqs
    step = xs // STEPS

    def spec(array, start, which):
        skip = which * STEPS if array.shape[2] > xs else 0
        return pl.BlockSpec(
            (2, 1, step) + array.shape[3:], lambda f, x: (0, f + first - start, x + skip, 0, 0)
        )

    return pl.pallas_call(
        products_kernel,
        grid=(count, STEPS),
        in_specs=[pl.BlockSpec(memory_space=pltpu.SMEM)]
        + [spec(*block, i % 2) for i, block in enumerate(zip(arrays, starts))],
        out_specs=pl.BlockSpec((8, 1, 2 * shots + PAD, recv // 4), lambda f, x: (0, f, 0, 0)),
        out_shape=jax.ShapeDtypeStruct((8, count, 2 * shots + PAD, recv // 4), jnp.int16),
        scratch_shapes=[pltpu.VMEM((4 * shots, recv), jnp.float32)],
        compiler_params=pltpu.CompilerParams(vmem_limit_bytes=58 * 2**20),
        cost_estimate=pl.CostEstimate(
            flops=COST * count * 2 * (4 * shots) * (2 * rows) * recv,
            bytes_accessed=2**20,
            transcendentals=0,
        ),
        name="products",
    )(place, *arrays)


def finish_kernel(terms, *refs):
    out = refs[-1]
    shots = out.shape[3]

    def wide(values):
        return values.astype(jnp.int32).astype(jnp.float32)

    for core in range(2):
        sums = [jnp.zeros(out.shape[3:], jnp.float32) for _ in range(2)]
        for chip in range(4):
            source = 2 * chip + core
            level = wide(terms[source, 0, 2 * shots : 2 * shots + PAD])[:1]
            unit = jnp.exp2(level * (1.0 / LOG)) * (1.0 / TOP)
            for part in range(2):
                steps = wide(terms[source, 0, part * shots : (part + 1) * shots])
                sums[part] = sums[part] + steps * unit
        for part in range(2):
            out[part, core, 0] = sums[part].astype(out.dtype)


def finish(terms, freqs, count, before):
    first, size = freqs
    rows, width = terms.shape[2:]
    shots = (rows - PAD) // 2
    done = [] if before is None else [before]
    return pl.pallas_call(
        finish_kernel,
        grid=(size,),
        in_specs=[pl.BlockSpec((8, 1, rows, width), lambda f: (0, f, 0, 0))]
        + [pl.BlockSpec(memory_space=pl.ANY)] * len(done),
        out_specs=pl.BlockSpec((2, 2, 1, shots, width), lambda f: (0, 0, f + first, 0, 0)),
        out_shape=jax.ShapeDtypeStruct((2, 2, count, shots, width), jnp.bfloat16),
        input_output_aliases={1: 0} if done else {},
        compiler_params=pltpu.CompilerParams(vmem_limit_bytes=16 * 2**20),
        name="finish",
    )(terms, *done)


def keep_live(live, kept):
    xs, pts, recv = kept.shape
    rows = lax.broadcasted_iota(jnp.int32, (pts, pts), 0)
    diagonal = rows == lax.broadcasted_iota(jnp.int32, (pts, pts), 1)
    receiver = lax.broadcasted_iota(jnp.int32, (pts, recv), 1).astype(jnp.float32)
    for x in range(xs):
        row = jnp.broadcast_to(live[x : x + 1, :].astype(jnp.float32), (pts, pts))
        column = jnp.sum(jnp.where(diagonal, row, 0.0), axis=1, keepdims=True)
        kept[x] = (receiver < column).astype(jnp.float32).astype(kept.dtype)


def keep_inside(first_point, aperture, inside):
    inline = first_point + lax.broadcasted_iota(jnp.int32, inside.shape, 0)
    within = (inline >= aperture[0:1, :]) & (inline < aperture[1:2, :])
    inside[...] = within.astype(jnp.float32).astype(inside.dtype)


def put_masked(source, piece, to, at, offset, inside):
    pts = inside.shape[0] // 5
    kept = inside[offset * pts : (offset + 1) * pts, :]
    for part in range(2):
        for freq in range(source.shape[1]):
            to[part, freq, :, at * pts : (at + 1) * pts, :] = (
                source[part, freq, :, piece * pts : (piece + 1) * pts, :] * kept
            )


def first_kernel(place, live, aperture, *refs):
    mine, others, low, high, other_shots = refs[:5]
    early, leaving, crossing, cross_leaving, shots_leaving, kept, inside = refs[5:]

    @pl.when(pl.program_id(0) == 0)
    def _():
        keep_live(live, kept)
        keep_inside(first_of(place, inside.shape[0] // 5), aperture, inside)
        for part in range(2):
            for freq in range(early.shape[1]):
                early[part, freq] = mine[part, freq] * kept[...]

    for part in range(2):
        for freq in range(leaving.shape[1]):
            leaving[part, freq] = others[part, freq] * kept[...]
    put_masked(low, 0, crossing, 0, 1, inside)
    put_masked(high, 0, crossing, 1, 3, inside)
    for k in range(5):
        put_masked(other_shots, k, cross_leaving if k % 2 else shots_leaving, k // 2, k, inside)


def second_kernel(place, aperture, below, here, above, staying, inside):
    @pl.when(pl.program_id(0) == 0)
    def _():
        keep_inside(first_of(place, inside.shape[0] // 5), aperture, inside)

    for k, source in enumerate((below, here, above)):
        put_masked(source, 0, staying, k, 2 * k, inside)


def prepare(place, gathers, live, shots, aperture):
    freqs, xs, pts, recv = gathers.shape[1:]
    spread, width = shots.shape[3:]
    count = freqs // 2
    steps = count // FIRST

    def block(rows, columns):
        return (2, FIRST, xs, rows, columns)

    def source(other, at, rows):
        def index(i, place):
            return (0, (core_of(place) ^ other) * steps + i, 0, at, 0)

        return pl.BlockSpec(block(rows, width), index)

    def result(rows, columns):
        return pl.BlockSpec(block(rows, columns), lambda i, place: (0, i, 0, 0, 0))

    sizes = (2 * pts, 2 * pts, 3 * pts)
    return pl.pallas_call(
        first_kernel,
        grid_spec=pltpu.PrefetchScalarGridSpec(
            num_scalar_prefetch=1,
            grid=(steps,),
            in_specs=[
                pl.BlockSpec((xs, pts), lambda i, place: (0, 0)),
                pl.BlockSpec((2, width), lambda i, place: (0, 0)),
                pl.BlockSpec(block(pts, recv), lambda i, place: (0, core_of(place) * steps, 0, 0, 0)),
                pl.BlockSpec(
                    block(pts, recv), lambda i, place: (0, (1 - core_of(place)) * steps + i, 0, 0, 0)
                ),
                source(0, 1, pts),
                source(0, 3, pts),
                source(1, 0, spread),
            ],
            out_specs=[
                pl.BlockSpec(block(pts, recv), lambda i, place: (0, 0, 0, 0, 0)),
                result(pts, recv),
            ]
            + [result(rows, width) for rows in sizes],
            scratch_shapes=[
                pltpu.VMEM((xs, pts, recv), gathers.dtype),
                pltpu.VMEM((spread, width), shots.dtype),
            ],
        ),
        out_shape=[
            jax.ShapeDtypeStruct((2, FIRST, xs, pts, recv), gathers.dtype),
            jax.ShapeDtypeStruct((2, count, xs, pts, recv), gathers.dtype),
        ]
        + [jax.ShapeDtypeStruct((2, count, xs, rows, width), shots.dtype) for rows in sizes],
        compiler_params=pltpu.CompilerParams(vmem_limit_bytes=58 * 2**20),
        cost_estimate=pl.CostEstimate(flops=0, bytes_accessed=13 * 2**20, transcendentals=0),
        name="prepare",
    )(place, live, aperture, gathers, gathers, shots, shots, shots)


def stay(place, shots, aperture):
    freqs, xs, spread, width = shots.shape[1:]
    count, pts = freqs // 2, spread // 5
    steps = count // FIRST

    def source(at):
        return pl.BlockSpec(
            (2, FIRST, xs, pts, width), lambda i, place: (0, core_of(place) * steps + i, 0, at, 0)
        )

    return pl.pallas_call(
        second_kernel,
        grid_spec=pltpu.PrefetchScalarGridSpec(
            num_scalar_prefetch=1,
            grid=(steps,),
            in_specs=[pl.BlockSpec((2, width), lambda i, place: (0, 0))]
            + [source(at) for at in (0, 2, 4)],
            out_specs=pl.BlockSpec(
                (2, FIRST, xs, 3 * pts, width), lambda i, place: (0, i, 0, 0, 0)
            ),
            scratch_shapes=[pltpu.VMEM((spread, width), shots.dtype)],
        ),
        out_shape=jax.ShapeDtypeStruct((2, count, xs, 3 * pts, width), shots.dtype),
        compiler_params=pltpu.CompilerParams(vmem_limit_bytes=58 * 2**20),
        cost_estimate=pl.CostEstimate(flops=0, bytes_accessed=3 * 2**20, transcendentals=0),
        name="stay",
    )(place, aperture, shots, shots, shots)


def on_device(surface_gathers, source_gathers, aperture, live):
    freqs_here, _, pts, _ = surface_gathers.shape[1:]
    spread = source_gathers.shape[4]
    half, core = lax.axis_index("half"), lax.axis_index("core")
    count = freqs_here // 2
    place = lax.axis_index(SHOT + XLINE).astype(jnp.int32).reshape(1)

    shots = source_gathers.transpose(0, 1, 3, 4, 2)
    early, leaving, crossing, cross_leaving, shots_leaving = prepare(
        place, surface_gathers, live, shots, aperture.T
    )
    below_early, above_early = shifted(early, 1), shifted(early, -1)
    gathers = swapped(leaving, "core")
    others = swapped(shots_leaving, "core")
    cross = [(swapped(crossing, "half"), 0), (swapped(cross_leaving, ("half", "core")), 0)]
    gathers, surface_gathers = lax.optimization_barrier((gathers, surface_gathers))
    others, shots = lax.optimization_barrier((others, shots))
    staying = stay(place, shots, aperture.T)
    heard = lax.broadcasted_iota(jnp.int32, surface_gathers.shape[2:], 2) < live[:, :, None]
    late = lax.dynamic_slice_in_dim(surface_gathers, core * count + FIRST, count - FIRST, 1)
    late = jnp.where(heard, late, jnp.zeros((), late.dtype))
    early_too = gathers[:, :FIRST]
    below_too, above_too = shifted(early_too, 1), shifted(early_too, -1)
    own = [(staying, 0), (others, 0)]
    here, below, above = [[(early, 0), (gathers, 0)]], [], []
    arrived = [below_early, above_early]
    spans = [(0, FIRST)] + [(i, 1) for i in range(FIRST, count)]
    for i, (first, size) in enumerate(spans):
        if i:
            block = jnp.concatenate(
                [late[:, first - FIRST : first - FIRST + 1], gathers[:, first : first + 1]], axis=2
            )
            if i == 1:
                block, arrived = lax.optimization_barrier((block, arrived))
                block_after = [below_too, above_too]
            else:
                block, block_after[0] = lax.optimization_barrier((block, block_after[0]))
                below.insert(0, [(arrived[0], 0), (block_after[0], 0)])
                above.insert(0, [(arrived[1], 0), (block_after[1], 0)])
            here.append([(block, first)])
            below.append([(shifted(block, 1), first)])
            above.append([(shifted(block, -1), first)])
    partial = [
        products(place, spans[i], below[i], here[i], above[i], own, cross)
        for i in range(len(spans))
    ]
    predicted = None
    for i, freqs in enumerate(spans):
        terms = lax.all_to_all(partial[i], RING, 0, 0, tiled=True)
        if i + 1 < len(spans):
            terms, partial[i + 1] = lax.optimization_barrier((terms, partial[i + 1]))
        predicted = finish(terms, freqs, count, predicted)
    return predicted.reshape((2, freqs_here) + predicted.shape[3:])


def solution(mesh):
    fine = Mesh(
        mesh.devices.reshape(mesh.shape["shot"] // 2, 2, mesh.shape["xline"] // 2, 2),
        SHOT + XLINE,
    )
    return jax.shard_map(
        on_device,
        mesh=fine,
        in_specs=(
            P(None, None, XLINE, SHOT, None),
            P(None, None, SHOT, XLINE, None),
            P(SHOT, None),
            P(XLINE, SHOT),
        ),
        out_specs=P(None, None, SHOT, XLINE),
        check_vma=False,
    )
```
